512 devices in a mesh: snode: 64 (over x, z, core), grp: 8 (over y).
Axes of the slice: x: 4, y: 8, z: 8, core: 2. Of those that a mesh axis runs over, the one named last changes fastest.
Arguments:
- ancestor_inverse: float32 [256, 256, 256], P('snode', 'grp'), may hold values from -6 to 6
- panel: float32 [64, 8, 256, 256], P('snode', None, 'grp'), may hold values from -0.125 to 0.125
- need_list: int32 [64, 8, 8], P('snode'), may hold values from 0 to 255, as said below
- diag_factor: float32 [64, 256, 256], P('snode', 'grp'), may hold values from -6 to 6
Outputs:
- off_inverse: float32 [64, 8, 256, 256], P('snode', None, 'grp')
- diag_inverse: float32 [64, 256, 256], P('snode', 'grp')
The draws below stay inside these ranges and needn't reach their ends.
Inputs may be any that keep to these rules, and one draw needn't show every extreme that they name: `need_list`: the entries of the supernodes of one index of snode name exactly 16 distinct blocks. Of these, at most 2 are held by any one owner o (block ids 4 * o to 4 * o + 3); at least one owner holds exactly 2, and other owners may hold 2 as well.
All inputs are finite; a program needn't handle non-finite values.
Results may differ from the reference program's by a relative error of at most 0.00007.
Values sent between devices are 32-bit elements; how exact they have to be, the bound alone decides.
No kernel may reach another device: no remote copies, remote signals or barrier semaphores. Data moves between devices by JAX's collectives and lax.ppermute only.
A program may use at most 64 MiB of HBM per device.

```python
import jax
import jax.numpy as jnp
from jax import lax

W = 256
K = 8
SN_DEV = 1
BLK_DEV = 4
SN_TOT = 64
NBLK = 256
N_SNODE = 64


def draw_need_list(key, part):
    key = jax.random.fold_in(key, 7)
    count = SN_DEV * K * K
    distinct = count // 4
    capacity = max(2, (distinct + N_SNODE - 1) // N_SNODE)
    other_slots = (N_SNODE - 1) * capacity

    def one_device(device):
        dev_key = jax.random.fold_in(key, device)
        key_hot, key_pick, key_within, key_cover, key_order = jax.random.split(dev_key, 5)
        hottest = jax.random.randint(key_hot, (), 0, N_SNODE)
        chosen = jax.random.permutation(key_pick, other_slots)[:distinct - capacity]
        other_owner = (hottest + 1 + chosen // capacity) % N_SNODE
        other_rank = chosen % capacity
        owners = jnp.concatenate([jnp.full((capacity,), hottest, jnp.int32), other_owner.astype(jnp.int32)])
        ranks = jnp.concatenate([jnp.arange(capacity, dtype=jnp.int32), other_rank.astype(jnp.int32)])
        orders = jax.vmap(lambda k: jax.random.permutation(k, BLK_DEV))(jax.random.split(key_within, N_SNODE))
        within = orders[owners, ranks]
        ids = owners * BLK_DEV + within
        picks = jnp.concatenate([jnp.arange(distinct, dtype=jnp.int32), jax.random.randint(key_cover, (count - distinct,), 0, distinct)])
        picks = picks[jax.random.permutation(key_order, count)]
        return ids[picks].reshape(SN_DEV, K, K)
    drawn = jax.vmap(one_device)(jnp.arange(N_SNODE))
    return drawn.reshape(SN_TOT, K, K).astype(jnp.int32)


def block_levels(own_key, shape, cuts, low, largest):
    loudness, own = 1.0, jax.random.fold_in(own_key, 6)
    for dim, shards_of in cuts:
        steps = jnp.exp(jax.random.uniform(jax.random.fold_in(own, dim), (shards_of,), jnp.float32, low / len(cuts), largest / len(cuts)))
        loudness = loudness * jnp.repeat(steps, shape[dim] // shards_of).reshape([-1 if axis == dim else 1 for axis in range(len(shape))])
    return loudness


def centred(rng, dims, width, reach, shards=(), held_as=jnp.bfloat16):
    loudness = block_levels(rng, dims, shards, -0.22, 0.18) if shards else 1.0
    values = jax.random.normal(rng, dims, jnp.float32) * width * loudness
    return jnp.minimum(jnp.maximum(values, -reach), reach).astype(held_as)


def setup_inputs(seed: int = 0) -> dict:
    seeds = jax.random.split(jax.random.key(seed), 5)
    ancestor_inverse = centred(seeds[0], (NBLK, W, W), 1.0, 6.0, ((0, 64), (1, 8)), jnp.float32)
    panel = centred(seeds[1], (SN_TOT, K, W, W), (K * W) ** -0.5, 0.125, ((0, 64), (2, 8)), jnp.float32)
    need_list = draw_need_list(jax.random.fold_in(seeds[4], 71), 0)
    diag_factor = centred(seeds[3], (SN_TOT, W, W), 1.0, 6.0, ((0, 64), (1, 8)), jnp.float32)
    return dict(ancestor_inverse=ancestor_inverse, panel=panel, need_list=need_list, diag_factor=diag_factor)


def reference(ancestor_inverse, panel, need_list, diag_factor):
    def one_node(items):
        needed, panel_node, diag_node = items
        blocks = ancestor_inverse[needed.reshape(-1)].reshape(K, K, W, W)
        off_block = -jnp.einsum("abij,bjk->aik", blocks, panel_node, precision=lax.Precision.HIGHEST)
        update = jnp.einsum("aji,ajk->ik", panel_node, off_block, precision=lax.Precision.HIGHEST)
        return off_block, diag_node - update

    off_inverse, diag_inverse = lax.map(one_node, (need_list, panel, diag_factor))
    return off_inverse, diag_inverse
```

```python
import jax
import jax.numpy as jnp
from jax import lax
from jax.experimental import pallas as pl
from jax.experimental.pallas import tpu as pltpu
from jax.sharding import PartitionSpec as P

NX, NZ, NC = 4, 8, 2
SLOTS = 16


def node(x, z, c):
    return ((x % NX) * NZ + z % NZ) * NC + c


EVERY = [(x, z, c) for x in range(NX) for z in range(NZ) for c in range(NC)]
TWIN = [(node(x, z, c), node(x, z, 1 - c)) for x, z, c in EVERY]
ROUND = [(node(x, z, c), node(x, z + 1 - 2 * c, c)) for x, z, c in EVERY]
X_ONE = [(node(x, z, c), node(x ^ 1, z, c)) for x, z, c in EVERY]
X_TWO = [(node(x, z, c), node(x ^ 2, z, c)) for x, z, c in EVERY]
X_LINES = [[node(x, z, c) for x in range(NX)] for z in range(NZ) for c in range(NC)]


def split(v):
    high = v.astype(jnp.bfloat16)
    return high, (v - high.astype(jnp.float32)).astype(jnp.bfloat16)


def dot3(a, b, dims):
    (ah, al), (bh, bl) = split(a), split(b)
    dot = lambda u, v: lax.dot_general(u, v, (dims, ((), ())), preferred_element_type=jnp.float32)
    return dot(ah, bh) + (dot(ah, bl) + dot(al, bh))


def products(pick_ref, pool_ref, whole_ref, own_ref, off_ref, update_ref):
    kcount, rows, width = own_ref.shape
    total = jnp.zeros((kcount * rows, width), jnp.float32)
    for b in range(kcount):
        left = jnp.concatenate([pool_ref[pick_ref[a * kcount + b]] for a in range(kcount)], axis=0)
        total += dot3(left, whole_ref[b], ((1,), (0,)))
    off = -total
    off_ref[...] = off.reshape(off_ref.shape)
    own = own_ref[...].reshape(kcount * rows, width)
    update_ref[...] = dot3(own, off, ((0,), (0,))).reshape(update_ref.shape)


def per_device(ancestor_inverse, panel, need_list, diag_factor):
    _, kcount, rows, width = panel.shape
    held = ancestor_inverse.shape[0]
    here = lax.axis_index("snode")
    x, z, c = here // (NZ * NC), here // NC % NZ, here % NC

    wanted = need_list.reshape(-1)
    ids = jnp.arange(NX * NZ * NC * held, dtype=jnp.int32)
    present = jnp.any(wanted[:, None] == ids[None, :], axis=0)
    slot = jnp.sum((present[None, :] & (ids[None, :] < wanted[:, None])).astype(jnp.int32), axis=1)
    order = jnp.arange(SLOTS, dtype=jnp.int32)
    distinct = jnp.max(jnp.where(slot[None, :] == order[:, None], wanted[None, :], 0), axis=1)

    pair = jnp.stack([distinct, lax.ppermute(distinct, "snode", X_ONE)])
    lists = jnp.concatenate([pair, lax.ppermute(pair, "snode", X_TWO)])

    whole = lax.all_gather(panel, "grp", axis=2, tiled=True)

    chip = jnp.concatenate([ancestor_inverse, lax.ppermute(ancestor_inverse, "snode", TWIN)])
    passed, ring = chip, []
    for step in range(NZ // 2):
        passed = lax.ppermute(passed if step < NZ // 2 - 1 else passed[:held], "snode", ROUND)
        ring.append(passed)
    ring = jnp.concatenate(ring)
    pool = jnp.concatenate([chip, ring, lax.ppermute(ring, "snode", TWIN)])

    asked = lists[jnp.arange(NX) ^ x]
    owner, k = asked // held, asked % held
    oz, oc = owner // NC % NZ, owner % NC
    dz = (oz - z) % NZ
    holder = jnp.where(dz == NZ // 2, oc, (dz < NZ // 2).astype(jnp.int32))
    step = jnp.where(dz < NZ // 2, dz, NZ - dz)
    inside = jnp.where(dz == NZ // 2, (step - 1) * 2 * held, (step - 1) * 2 * held + (oc ^ holder) * held) + k
    start = jnp.where(holder == c, 2 * held, 2 * held + ring.shape[0])
    place = jnp.where(dz == 0, (oc ^ c) * held + k, start + inside)
    place = jnp.where(owner // (NC * NZ) == x, place, 0)
    answers = lax.all_to_all(
        pool[place], "snode", split_axis=0, concat_axis=0, tiled=True, axis_index_groups=X_LINES
    )
    fetched = answers.reshape(NX * SLOTS, rows, width)
    pick = wanted // (held * NC * NZ) * SLOTS + slot

    vmem = pl.BlockSpec(memory_space=pltpu.VMEM)
    off, update = pl.pallas_call(
        products,
        out_shape=(
            jax.ShapeDtypeStruct((kcount, rows, width), jnp.float32),
            jax.ShapeDtypeStruct((width // rows, rows, width), jnp.float32),
        ),
        in_specs=[pl.BlockSpec(memory_space=pltpu.SMEM), vmem, vmem, vmem],
        out_specs=(vmem, vmem),
        compiler_params=pltpu.CompilerParams(vmem_limit_bytes=32 * 1024 * 1024),
        cost_estimate=pl.CostEstimate(flops=2_000_000_000, bytes_accessed=5_000_000, transcendentals=0),
    )(pick, fetched, whole[0], panel[0])
    parts = lax.all_to_all(update, "grp", split_axis=0, concat_axis=0, tiled=True)
    return off[None], diag_factor - jnp.sum(parts, axis=0)[None]


def solution(mesh):
    return jax.shard_map(
        per_device,
        mesh=mesh,
        in_specs=(
            P("snode", "grp", None),
            P("snode", None, "grp", None),
            P("snode", None, None),
            P("snode", "grp", None),
        ),
        out_specs=(P("snode", None, "grp", None), P("snode", "grp", None)),
        check_vma=False,
    )
```

```python
import jax
import jax.numpy as jnp
from jax import lax
from jax.experimental import pallas as pl
from jax.experimental.pallas import tpu as pltpu
from jax.sharding import PartitionSpec as P

NX, NZ, NC, NY = 4, 8, 2, 8
SLOTS = 16
HALF = 4


def node(x, z, c):
    return ((x % NX) * NZ + z % NZ) * NC + c


EVERY = [(x, z, c) for x in range(NX) for z in range(NZ) for c in range(NC)]
TWIN = [(node(x, z, c), node(x, z, 1 - c)) for x, z, c in EVERY]
Z_ROUND = [(node(x, z, c), node(x, z + 1 - 2 * c, c)) for x, z, c in EVERY]
Y_ROUND = [
    (node(x, z, c) * NY + y, node(x, z, c) * NY + (y + 1 - 2 * c) % NY) for x, z, c in EVERY for y in range(NY)
]
X_ONE = [(node(x, z, c), node(x ^ 1, z, c)) for x, z, c in EVERY]
X_TWO = [(node(x, z, c), node(x ^ 2, z, c)) for x, z, c in EVERY]
X_LINES = [[node(x, z, c) for x in range(NX)] for z in range(NZ) for c in range(NC)]
VMEM = pl.BlockSpec(memory_space=pltpu.VMEM)
SMEM = pl.BlockSpec(memory_space=pltpu.SMEM)
PARAMS = pltpu.CompilerParams(vmem_limit_bytes=32 * 1024 * 1024)


def split(v):
    high = v.astype(jnp.bfloat16)
    return high, (v - high.astype(jnp.float32)).astype(jnp.bfloat16)


def dot3(a, b, dims):
    (ah, al), (bh, bl) = a, b
    dot = lambda u, v: lax.dot_general(u, v, (dims, ((), ())), preferred_element_type=jnp.float32)
    return dot(ah, bh) + (dot(ah, bl) + dot(al, bh))


def collect(place_ref, *refs):
    *pieces, answers_ref, pool_ref = refs
    at = 0
    for piece in pieces:
        count = piece.shape[0]
        pool_ref[at : at + count] = piece[...]
        at += count

    def one(s, carry):
        answers_ref[s] = pool_ref[place_ref[s]]
        return carry

    lax.fori_loop(0, answers_ref.shape[0], one, 0, unroll=4)


def assemble(rows_ref, own_ref, first_ref, *refs):
    *rest, high_ref, low_ref = refs
    leads, lags = rest[: HALF - 1], rest[HALF - 1 :]
    count, rows, _ = own_ref.shape
    pieces = [own_ref, first_ref] + [ref.at[pl.ds(0, count)] for ref in leads] + list(lags)
    for number, piece in enumerate(pieces):
        start = pl.multiple_of(rows_ref[number], rows)
        high, low = split(piece[...])
        high_ref[:, pl.ds(start, rows), :] = high
        low_ref[:, pl.ds(start, rows), :] = low


def products(pick_ref, fetched_ref, high_ref, low_ref, own_ref, off_ref, update_ref):
    kcount, rows, width = own_ref.shape
    total = jnp.zeros((kcount * rows, width), jnp.float32)
    for b in range(kcount):
        left = jnp.concatenate([fetched_ref[pick_ref[a * kcount + b]] for a in range(kcount)], axis=0)
        total += dot3(split(left), (high_ref[b], low_ref[b]), ((1,), (0,)))
    off = -total
    off_ref[...] = off.reshape(off_ref.shape)
    own = own_ref[...].reshape(kcount * rows, width)
    update_ref[...] = dot3(split(own), split(off), ((0,), (0,))).reshape(update_ref.shape)


def per_device(ancestor_inverse, panel, need_list, diag_factor):
    _, kcount, rows, width = panel.shape
    held = ancestor_inverse.shape[0]
    here, y = lax.axis_index("snode"), lax.axis_index("grp")
    x, z, c = here // (NZ * NC), here // NC % NZ, here % NC
    own = panel[0]
    twin = lambda v: lax.ppermute(v, "snode", TWIN)
    z_on = lambda v: lax.ppermute(v, "snode", Z_ROUND)
    y_on = lambda v: lax.ppermute(v, ("snode", "grp"), Y_ROUND)

    other = twin(ancestor_inverse)
    ring = [z_on(ancestor_inverse)]
    message = jnp.concatenate([ring[0], other])
    for _ in range(HALF - 1):
        message = z_on(message)
        ring.append(message)
    pieces = [ancestor_inverse, other] + ring + [twin(piece) for piece in ring]

    lead = y_on(own)
    message = jnp.concatenate([lead, twin(own)])
    both = []
    for _ in range(HALF - 1):
        message = y_on(message)
        both.append(message)
    lags = [twin(message[kcount:]) for message in both]

    wanted = need_list.reshape(-1)
    ids = jnp.arange(NX * NZ * NC * held, dtype=jnp.int32)
    present = jnp.any(wanted[:, None] == ids[None, :], axis=0)
    slot = jnp.sum((present[None, :] & (ids[None, :] < wanted[:, None])).astype(jnp.int32), axis=1)
    order = jnp.arange(SLOTS, dtype=jnp.int32)
    distinct = jnp.max(jnp.where(slot[None, :] == order[:, None], wanted[None, :], 0), axis=1)
    pair = jnp.stack([distinct, lax.ppermute(distinct, "snode", X_ONE)])
    lists = jnp.concatenate([pair, lax.ppermute(pair, "snode", X_TWO)])

    asked = lists[jnp.arange(NX) ^ x]
    owner, k = asked // held, asked % held
    oz, oc = owner // NC % NZ, owner % NC
    dz = (oz - z) % NZ
    holder = jnp.where(dz == HALF, oc, (dz < HALF).astype(jnp.int32))
    far = jnp.where(dz < HALF, dz, NZ - dz)
    lag = (oc != holder).astype(jnp.int32)
    arrived = far + lag
    inside = jnp.where(arrived == 1, 0, held + (arrived - 2) * 2 * held + lag * held) + k
    count = held + (HALF - 1) * 2 * held
    start = 2 * held + jnp.where(holder == c, 0, count)
    place = jnp.where(dz == 0, (oc ^ c) * held + k, start + inside)
    place = jnp.where(owner // (NC * NZ) == x, place, 0)

    block = (rows, width)
    answers = pl.pallas_call(
        collect,
        out_shape=jax.ShapeDtypeStruct((NX * SLOTS,) + block, jnp.float32),
        in_specs=[SMEM] + [VMEM] * len(pieces),
        out_specs=VMEM,
        scratch_shapes=[pltpu.VMEM((2 * held + 2 * count,) + block, jnp.float32)],
        compiler_params=PARAMS,
        cost_estimate=pl.CostEstimate(flops=0, bytes_accessed=4_000_000, transcendentals=0),
    )(place.reshape(-1), *pieces)
    fetched = lax.all_to_all(
        answers.reshape((NX, SLOTS) + block), "snode", split_axis=0, concat_axis=0, tiled=True, axis_index_groups=X_LINES
    ).reshape((NX * SLOTS,) + block)

    way = 2 * c - 1
    steps = jnp.array([0, 1, 2, 3, 4, -1, -2, -3], jnp.int32)
    high, low = pl.pallas_call(
        assemble,
        out_shape=(jax.ShapeDtypeStruct((kcount, NY * rows, width), jnp.bfloat16),) * 2,
        in_specs=[SMEM] + [VMEM] * (2 + len(both) + len(lags)),
        out_specs=(VMEM, VMEM),
        compiler_params=PARAMS,
        cost_estimate=pl.CostEstimate(flops=0, bytes_accessed=4_000_000, transcendentals=0),
    )((y + way * steps) % NY * rows, own, lead, *both, *lags)

    pick = wanted // (held * NC * NZ) * SLOTS + slot
    off, update = pl.pallas_call(
        products,
        out_shape=(
            jax.ShapeDtypeStruct((kcount,) + block, jnp.float32),
            jax.ShapeDtypeStruct((NY,) + block, jnp.float32),
        ),
        in_specs=[SMEM] + [VMEM] * 4,
        out_specs=(VMEM, VMEM),
        compiler_params=PARAMS,
        cost_estimate=pl.CostEstimate(flops=1_000_000_000, bytes_accessed=5_000_000, transcendentals=0),
    )(pick, fetched, high, low, own)
    parts = lax.all_to_all(update, "grp", split_axis=0, concat_axis=0, tiled=True)
    return off[None], diag_factor - jnp.sum(parts, axis=0)[None]


def solution(mesh):
    return jax.shard_map(
        per_device,
        mesh=mesh,
        in_specs=(
            P("snode", "grp", None),
            P("snode", None, "grp", None),
            P("snode", None, None),
            P("snode", "grp", None),
        ),
        out_specs=(P("snode", None, "grp", None), P("snode", "grp", None)),
        check_vma=False,
    )
```

```python
import jax
import jax.numpy as jnp
from jax import lax
from jax.experimental import pallas as pl
from jax.experimental.pallas import tpu as pltpu
from jax.sharding import PartitionSpec as P

NX, NZ, NC, NY = 4, 8, 2, 8
SLOTS = 16
HALF = NY // 2


def node(x, z, c):
    return ((x % NX) * NZ + z % NZ) * NC + c


EVERY = [(x, z, c) for x in range(NX) for z in range(NZ) for c in range(NC)]
TWIN = [(node(x, z, c), node(x, z, 1 - c)) for x, z, c in EVERY]
Y_UP = [(y, (y + 1) % NY) for y in range(NY)]
Y_DOWN = [(y, (y - 1) % NY) for y in range(NY)]
X_ONE = [(node(x, z, c), node(x ^ 1, z, c)) for x, z, c in EVERY]
X_TWO = [(node(x, z, c), node(x ^ 2, z, c)) for x, z, c in EVERY]
Z_LINES = [[node(x, z, c) for z in range(NZ)] for x in range(NX) for c in range(NC)]
X_LINES = [[node(x, z, c) for x in range(NX)] for z in range(NZ) for c in range(NC)]
VMEM = pl.BlockSpec(memory_space=pltpu.VMEM)
ANY = pl.BlockSpec(memory_space=pl.ANY)
SMEM = pl.BlockSpec(memory_space=pltpu.SMEM)
PARAMS = pltpu.CompilerParams(vmem_limit_bytes=12 * 1024 * 1024)


def split(v):
    high = v.astype(jnp.bfloat16)
    return high, (v - high.astype(jnp.float32)).astype(jnp.bfloat16)


def dot3(a, b, dims):
    (ah, al), (bh, bl) = a, b
    dot = lambda u, v: lax.dot_general(u, v, (dims, ((), ())), preferred_element_type=jnp.float32)
    return dot(ah, bh) + (dot(ah, bl) + dot(al, bh))


def collect(place_ref, mine_ref, twins_ref, answers_ref):
    count = mine_ref.shape[0]

    def one(s, carry):
        place = place_ref[s]
        inside = lax.rem(place, count)
        answers_ref[s] = jnp.where(place < count, mine_ref[inside], twins_ref[inside])
        return carry

    lax.fori_loop(0, answers_ref.shape[0], one, 0, unroll=8)


def products(slot_ref, from_ref, start_ref, fetched_ref, own_ref, *refs):
    *pieces, off_ref, update_ref, whole_ref, named_ref, sems = refs
    kcount, rows, width = own_ref.shape
    copies = []

    def fetch(source, target):
        copies.append(pltpu.make_async_copy(source, target, sems.at[len(copies)]))
        copies[-1].start()

    for number in range(SLOTS):
        fetch(fetched_ref.at[from_ref[number]], named_ref.at[number])
    ranges = [(0, kcount)] * (len(pieces) - 2) + [(0, kcount // 2), (kcount // 2, kcount)]
    for number, (piece, (begin, end)) in enumerate(zip(pieces, ranges)):
        start = pl.multiple_of(start_ref[min(number + 1, NY - 1)], rows)
        fetch(piece, whole_ref.at[pl.ds(begin, end - begin), pl.ds(start, rows), :])
    start = pl.multiple_of(start_ref[0], rows)
    whole_ref[:, pl.ds(start, rows), :] = own_ref[...]
    for copy in copies:
        copy.wait()

    total = jnp.zeros((kcount * rows, width), jnp.float32)
    for b in range(kcount):
        left = jnp.concatenate([named_ref[slot_ref[a * kcount + b]] for a in range(kcount)], axis=0)
        total += dot3(split(left), split(whole_ref[b]), ((1,), (0,)))
    off = -total
    off_ref[...] = off.reshape(off_ref.shape)
    own = own_ref[...].reshape(kcount * rows, width)
    update_ref[...] = dot3(split(own), split(off), ((0,), (0,))).reshape(update_ref.shape)


def per_device(ancestor_inverse, panel, need_list, diag_factor):
    _, kcount, rows, width = panel.shape
    held = ancestor_inverse.shape[0]
    here, y = lax.axis_index("snode"), lax.axis_index("grp")
    x, c = here // (NZ * NC), here % NC
    own = panel[0]
    block = (rows, width)

    wanted = need_list.reshape(-1)
    ids = jnp.arange(NX * NZ * NC * held, dtype=jnp.int32)
    present = jnp.any(wanted[:, None] == ids[None, :], axis=0)
    slot = jnp.sum((present[None, :] & (ids[None, :] < wanted[:, None])).astype(jnp.int32), axis=1)
    order = jnp.arange(SLOTS, dtype=jnp.int32)
    distinct = jnp.max(jnp.where(slot[None, :] == order[:, None], wanted[None, :], 0), axis=1)
    pair = jnp.stack([distinct, lax.ppermute(distinct, "snode", X_ONE)])
    lists = jnp.concatenate([pair, lax.ppermute(pair, "snode", X_TWO)])

    mine = lax.all_to_all(
        jnp.broadcast_to(ancestor_inverse[None], (NZ,) + ancestor_inverse.shape),
        "snode", split_axis=0, concat_axis=0, tiled=True, axis_index_groups=Z_LINES,
    ).reshape((NZ * held,) + block)
    up = down = own
    pieces = []
    for step in range(1, HALF + 1):
        last = step == HALF
        up = lax.ppermute(up[: kcount // 2] if last else up, "grp", Y_UP)
        down = lax.ppermute(down[kcount // 2 :] if last else down, "grp", Y_DOWN)
        pieces += [up, down]
        if step == 2:
            mine, lists, up, down = lax.optimization_barrier((mine, lists, up, down))
    twins = lax.ppermute(mine, "snode", TWIN)

    asked = lists[jnp.arange(NX) ^ x]
    owner, k = asked // held, asked % held
    place = owner // NC % NZ * held + k + jnp.where(owner % NC == c, 0, NZ * held)
    place = jnp.where(owner // (NC * NZ) == x, place, 0)

    answers = pl.pallas_call(
        collect,
        out_shape=jax.ShapeDtypeStruct((NX * SLOTS,) + block, jnp.float32),
        in_specs=[SMEM, VMEM, VMEM],
        out_specs=VMEM,
        compiler_params=PARAMS,
        cost_estimate=pl.CostEstimate(flops=0, bytes_accessed=4_000_000, transcendentals=0),
    )(place.reshape(-1), mine, twins)
    fetched = lax.all_to_all(
        answers.reshape((NX, SLOTS) + block), "snode", split_axis=0, concat_axis=0, tiled=True, axis_index_groups=X_LINES
    ).reshape((NX * SLOTS,) + block)

    starts = (y + jnp.array([0, -1, 1, -2, 2, -3, 3, HALF], jnp.int32)) % NY * rows
    off, update = pl.pallas_call(
        products,
        out_shape=(
            jax.ShapeDtypeStruct((kcount,) + block, jnp.float32),
            jax.ShapeDtypeStruct((NY,) + block, jnp.float32),
        ),
        in_specs=[SMEM] * 3 + [ANY, VMEM] + [ANY] * len(pieces),
        out_specs=(VMEM, VMEM),
        scratch_shapes=[
            pltpu.VMEM((kcount, NY * rows, width), jnp.float32),
            pltpu.VMEM((SLOTS,) + block, jnp.float32),
            pltpu.SemaphoreType.DMA((SLOTS + len(pieces),)),
        ],
        compiler_params=PARAMS,
        cost_estimate=pl.CostEstimate(flops=1_000_000_000, bytes_accessed=5_000_000, transcendentals=0),
    )(slot, distinct // (held * NC * NZ) * SLOTS + order, starts, fetched, own, *pieces)
    parts = lax.all_to_all(update, "grp", split_axis=0, concat_axis=0, tiled=True)
    return off[None], diag_factor - jnp.sum(parts, axis=0)[None]


def solution(mesh):
    return jax.shard_map(
        per_device,
        mesh=mesh,
        in_specs=(
            P("snode", "grp", None),
            P("snode", None, "grp", None),
            P("snode", None, None),
            P("snode", "grp", None),
        ),
        out_specs=(P("snode", None, "grp", None), P("snode", "grp", None)),
        check_vma=False,
    )
```

```python
import jax
import jax.numpy as jnp
from jax import lax
from jax.experimental import pallas as pl
from jax.experimental.pallas import tpu as pltpu
from jax.sharding import PartitionSpec as P

NX, NZ, NC, NY = 4, 8, 2, 8
SLOTS = 16
HALF = NY // 2


def node(x, z, c):
    return ((x % NX) * NZ + z % NZ) * NC + c


EVERY = [(x, z, c) for x in range(NX) for z in range(NZ) for c in range(NC)]
TWIN = [(node(x, z, c), node(x, z, 1 - c)) for x, z, c in EVERY]
Y_ROUND = [
    (node(x, z, c) * NY + y, node(x, z, c) * NY + (y + 1 - 2 * c) % NY) for x, z, c in EVERY for y in range(NY)
]
X_ONE = [(node(x, z, c), node(x ^ 1, z, c)) for x, z, c in EVERY]
X_TWO = [(node(x, z, c), node(x ^ 2, z, c)) for x, z, c in EVERY]
Z_LINES = [[node(x, z, c) for z in range(NZ)] for x in range(NX) for c in range(NC)]
X_LINES = [[node(x, z, c) for x in range(NX)] for z in range(NZ) for c in range(NC)]
VMEM = pl.BlockSpec(memory_space=pltpu.VMEM)
HBM = pl.BlockSpec(memory_space=pltpu.HBM)
SMEM = pl.BlockSpec(memory_space=pltpu.SMEM)
PARAMS = pltpu.CompilerParams(vmem_limit_bytes=12 * 1024 * 1024)


def split(v):
    high = v.astype(jnp.bfloat16)
    return high, (v - high.astype(jnp.float32)).astype(jnp.bfloat16)


def dot3(a, b, dims):
    (ah, al), (bh, bl) = a, b
    dot = lambda u, v: lax.dot_general(u, v, (dims, ((), ())), preferred_element_type=jnp.float32)
    return dot(ah, bh) + (dot(ah, bl) + dot(al, bh))


def repeat(block_ref, all_ref, sem):
    copies = [pltpu.make_async_copy(block_ref, all_ref.at[n], sem.at[n]) for n in range(all_ref.shape[0])]
    for copy in copies:
        copy.start()
    for copy in copies:
        copy.wait()


def collect(place_ref, mine_ref, twins_ref, answers_ref, picked_ref, sem):
    count = mine_ref.shape[0]
    readers, slots = answers_ref.shape[:2]
    for reader in range(readers):

        def one(s, carry):
            place = place_ref[reader * slots + s]
            inside = lax.rem(place, count)
            picked_ref[reader, s] = jnp.where(place < count, mine_ref[inside], twins_ref[inside])
            return carry

        lax.fori_loop(0, slots, one, 0, unroll=8)
        pltpu.make_async_copy(picked_ref.at[reader], answers_ref.at[reader], sem.at[reader]).start()
    for reader in range(readers):
        pltpu.make_async_copy(picked_ref.at[reader], answers_ref.at[reader], sem.at[reader]).wait()


def stage(own_ref, diag_ref, staged_ref):
    staged_ref[: own_ref.shape[0]] = own_ref[...]
    staged_ref[own_ref.shape[0]] = diag_ref[...]


def products(pick_ref, start_ref, fetched_ref, staged_ref, *refs):
    *pieces, off_ref, update_ref, whole_ref, sems = refs
    kcount, rows, _ = off_ref.shape
    copies = []

    starts = [pl.multiple_of(start_ref[number], rows) for number in range(NY)]
    messages = (len(pieces) - 1) // 2
    parts = [staged_ref.at[pl.ds(0, kcount)], pieces[0]] + [piece.at[pl.ds(0, kcount)] for piece in pieces[1 : 1 + messages]]
    parts += [piece.at[pl.ds(kcount, kcount)] for piece in pieces[1 + messages :]]
    for number, (part, start) in enumerate(zip(parts, starts)):
        copies.append(pltpu.make_async_copy(part, whole_ref.at[:, pl.ds(start, rows), :], sems.at[number]))
        copies[-1].start()
    for copy in copies:
        copy.wait()

    total = jnp.zeros((kcount * rows, whole_ref.shape[2]), jnp.float32)
    for b in range(kcount):
        left = jnp.concatenate([fetched_ref[pick_ref[a * kcount + b]] for a in range(kcount)], axis=0)
        total += dot3(split(left), split(whole_ref[b]), ((1,), (0,)))
    off_ref[...] = -total.reshape(off_ref.shape)
    own = staged_ref[:kcount].reshape(total.shape)
    update_ref[...] = dot3(split(own), split(total), ((0,), (0,))).reshape(update_ref.shape)
    update_ref[lax.div(starts[0], rows)] += staged_ref[kcount]


def per_device(ancestor_inverse, panel, need_list, diag_factor):
    _, kcount, rows, width = panel.shape
    held = ancestor_inverse.shape[0]
    here, y = lax.axis_index("snode"), lax.axis_index("grp")
    x, c = here // (NZ * NC), here % NC
    own = panel[0]
    block = (rows, width)

    wanted = need_list.reshape(-1)
    ids = jnp.arange(NX * NZ * NC * held, dtype=jnp.int32)
    present = jnp.any(wanted[:, None] == ids[None, :], axis=0)
    slot = jnp.sum((present[None, :] & (ids[None, :] < wanted[:, None])).astype(jnp.int32), axis=1)
    order = jnp.arange(SLOTS, dtype=jnp.int32)
    distinct = jnp.max(jnp.where(slot[None, :] == order[:, None], wanted[None, :], 0), axis=1)
    neighbour = lax.ppermute(distinct, "snode", X_ONE)
    pair = jnp.stack([distinct, neighbour])
    lists = jnp.concatenate([pair, lax.ppermute(pair, "snode", X_TWO)])

    copies = pl.pallas_call(
        repeat,
        out_shape=jax.ShapeDtypeStruct((NZ,) + ancestor_inverse.shape, jnp.float32),
        in_specs=[HBM],
        out_specs=HBM,
        scratch_shapes=[pltpu.SemaphoreType.DMA((NZ,))],
        compiler_params=PARAMS,
    )(ancestor_inverse)
    mine = lax.all_to_all(
        copies,
        "snode", split_axis=0, concat_axis=0, tiled=True, axis_index_groups=Z_LINES,
    ).reshape((NZ * held,) + block)
    on = lambda v: lax.ppermute(v, ("snode", "grp"), Y_ROUND)
    twin = lambda v: lax.ppermute(v, "snode", TWIN)
    lead = on(own)
    later, _ = lax.optimization_barrier((own, neighbour))
    passed = on(jnp.concatenate([lead, twin(later)]))
    mine, lists, passed = lax.optimization_barrier((mine, lists, passed))
    twins = twin(mine)
    staged = pl.pallas_call(
        stage,
        out_shape=jax.ShapeDtypeStruct((kcount + 1,) + block, jnp.float32),
        in_specs=[VMEM, VMEM],
        out_specs=VMEM,
        compiler_params=PARAMS,
    )(own, diag_factor[0])
    messages, swapped = [passed], []
    for step in range(HALF - 2):
        if step == 1:
            staged, messages[-1] = lax.optimization_barrier((staged, messages[-1]))
        following = on(messages[-1])
        before, following = lax.optimization_barrier((messages[-1], following))
        swapped.append(twin(before))
        messages.append(following)
    pieces = [lead] + messages + swapped + [twin(messages[-1])]

    asked = lists[jnp.arange(NX) ^ x]
    owner, k = asked // held, asked % held
    place = owner // NC % NZ * held + k + jnp.where(owner % NC == c, 0, NZ * held)
    place = jnp.where(owner // (NC * NZ) == x, place, 0)

    answers = pl.pallas_call(
        collect,
        out_shape=jax.ShapeDtypeStruct((NX, SLOTS) + block, jnp.float32),
        in_specs=[SMEM, VMEM, VMEM],
        out_specs=HBM,
        scratch_shapes=[pltpu.VMEM((NX, SLOTS) + block, jnp.float32), pltpu.SemaphoreType.DMA((NX,))],
        compiler_params=PARAMS,
        cost_estimate=pl.CostEstimate(flops=0, bytes_accessed=4_000_000, transcendentals=0),
    )(place.reshape(-1), mine, twins)
    fetched = lax.all_to_all(
        answers, "snode", split_axis=0, concat_axis=0, tiled=True, axis_index_groups=X_LINES
    ).reshape((NX * SLOTS,) + block)

    starts = (y + (2 * c - 1) * jnp.array([0, 1, 2, 3, 4, -1, -2, -3], jnp.int32)) % NY * rows
    off, update = pl.pallas_call(
        products,
        out_shape=(
            jax.ShapeDtypeStruct((kcount,) + block, jnp.float32),
            jax.ShapeDtypeStruct((NY,) + block, jnp.float32),
        ),
        in_specs=[SMEM] * 2 + [VMEM] * 2 + [HBM] * len(pieces),
        out_specs=(VMEM, VMEM),
        scratch_shapes=[pltpu.VMEM((kcount, NY * rows, width), jnp.float32), pltpu.SemaphoreType.DMA((NY,))],
        compiler_params=PARAMS,
        cost_estimate=pl.CostEstimate(flops=1_000_000_000, bytes_accessed=5_000_000, transcendentals=0),
    )(wanted // (held * NC * NZ) * SLOTS + slot, starts, fetched, staged, *pieces)
    parts = lax.all_to_all(update, "grp", split_axis=0, concat_axis=0, tiled=True)
    return off[None], jnp.sum(parts, axis=0)[None]


def solution(mesh):
    return jax.shard_map(
        per_device,
        mesh=mesh,
        in_specs=(
            P("snode", "grp", None),
            P("snode", None, "grp", None),
            P("snode", None, None),
            P("snode", "grp", None),
        ),
        out_specs=(P("snode", None, "grp", None), P("snode", "grp", None)),
        check_vma=False,
    )
```

```python
import jax
import jax.numpy as jnp
from jax import lax
from jax.experimental import pallas as pl
from jax.experimental.pallas import tpu as pltpu
from jax.sharding import PartitionSpec as P

NX, NZ, NC, NY = 4, 8, 2, 8
SLOTS = 16
FEW = 12
HALF = NY // 2


def node(x, z, c):
    return ((x % NX) * NZ + z % NZ) * NC + c


EVERY = [(x, z, c) for x in range(NX) for z in range(NZ) for c in range(NC)]
TWIN = [(node(x, z, c), node(x, z, 1 - c)) for x, z, c in EVERY]
Y_ROUND = [
    (node(x, z, c) * NY + y, node(x, z, c) * NY + (y + 1 - 2 * c) % NY) for x, z, c in EVERY for y in range(NY)
]
X_ONE = [(node(x, z, c), node(x ^ 1, z, c)) for x, z, c in EVERY]
X_TWO = [(node(x, z, c), node(x ^ 2, z, c)) for x, z, c in EVERY]
Z_LINES = [[node(x, z, c) for z in range(NZ)] for x in range(NX) for c in range(NC)]
X_LINES = [[node(x, z, c) for x in range(NX)] for z in range(NZ) for c in range(NC)]
VMEM = pl.BlockSpec(memory_space=pltpu.VMEM)
HBM = pl.BlockSpec(memory_space=pltpu.HBM)
SMEM = pl.BlockSpec(memory_space=pltpu.SMEM)
in_hbm = lambda v: pltpu.with_memory_space_constraint(v, pltpu.HBM)
in_vmem = lambda v: pltpu.with_memory_space_constraint(v, pltpu.VMEM)
PARAMS = pltpu.CompilerParams(vmem_limit_bytes=12 * 1024 * 1024)


def split(v):
    high = v.astype(jnp.bfloat16)
    return high, (v - high.astype(jnp.float32)).astype(jnp.bfloat16)


def dot3(a, b, dims):
    (ah, al), (bh, bl) = a, b
    dot = lambda u, v: lax.dot_general(u, v, (dims, ((), ())), preferred_element_type=jnp.float32)
    return dot(ah, bh) + (dot(ah, bl) + dot(al, bh))


def repeat(block_ref, all_ref, held_ref, sem, sems):
    copy = pltpu.make_async_copy(block_ref, held_ref, sem)
    copy.start()
    copy.wait()
    copies = [pltpu.make_async_copy(held_ref, all_ref.at[n], sems.at[n]) for n in range(all_ref.shape[0])]
    for copy in copies:
        copy.start()
    for copy in copies:
        copy.wait()


def collect(place_ref, mine_ref, twins_ref, few_ref, rest_ref, picked_ref, sem):
    count = mine_ref.shape[0]
    readers, few = few_ref.shape[:2]
    slots = few + rest_ref.shape[1]
    copies = []
    for target_ref, begin, end in ((few_ref, 0, few), (rest_ref, few, slots)):
        for reader in range(readers):

            def one(s, carry):
                place = place_ref[reader * slots + s]
                inside = lax.rem(place, count)
                picked_ref[reader, s] = jnp.where(place < count, mine_ref[inside], twins_ref[inside])
                return carry

            lax.fori_loop(begin, end, one, 0, unroll=4)
            source = picked_ref.at[reader, pl.ds(begin, end - begin)]
            copies.append(pltpu.make_async_copy(source, target_ref.at[reader], sem.at[len(copies)]))
            copies[-1].start()
    for copy in copies:
        copy.wait()


def stage(own_ref, diag_ref, staged_ref):
    staged_ref[: own_ref.shape[0]] = own_ref[...]
    staged_ref[own_ref.shape[0]] = diag_ref[...]


def assemble(start_ref, staged_ref, *refs):
    *pieces, whole_ref, raw_ref, sems = refs
    _, kcount, width, _ = whole_ref.shape
    rows = width // NY
    messages = (len(pieces) - 1) // 2
    parts = [piece.at[pl.ds(0, kcount)] for piece in pieces[: 1 + messages]]
    parts += [piece.at[pl.ds(kcount, kcount)] for piece in pieces[1 + messages :]]
    copies = [pltpu.make_async_copy(part, raw_ref.at[n], sems.at[n]) for n, part in enumerate(parts)]
    for copy in copies:
        copy.start()
    for number in range(NY):
        if number:
            copies[number - 1].wait()
        start = pl.multiple_of(start_ref[number], rows)
        high, low = split(raw_ref[number - 1] if number else staged_ref[:kcount])
        whole_ref[0, :, pl.ds(start, rows), :] = high
        whole_ref[1, :, pl.ds(start, rows), :] = low


def products(pick_ref, mine_ref, fetched_ref, extra_ref, staged_ref, whole_ref, off_ref, update_ref, held_ref, sem):
    kcount, rows, width = off_ref.shape
    count = fetched_ref.shape[0]

    def named(at):
        usual = fetched_ref[lax.min(at, count - 1)]
        return jnp.where(at < count, usual, extra_ref[lax.max(at - count, 0)])

    total = jnp.zeros((kcount * rows, width), jnp.float32)
    for b in range(kcount):
        left = jnp.concatenate([named(pick_ref[a * kcount + b]) for a in range(kcount)], axis=0)
        total += dot3(split(left), (whole_ref[0, b], whole_ref[1, b]), ((1,), (0,)))
    held_ref[...] = -total.reshape(off_ref.shape)
    copy = pltpu.make_async_copy(held_ref, off_ref, sem)
    copy.start()
    own = staged_ref[:kcount].reshape(total.shape)
    update_ref[...] = dot3(split(own), split(total), ((0,), (0,))).reshape(update_ref.shape)
    update_ref[mine_ref[0]] += staged_ref[kcount]
    copy.wait()


def per_device(ancestor_inverse, panel, need_list, diag_factor):
    _, kcount, rows, width = panel.shape
    held = ancestor_inverse.shape[0]
    here, y = lax.axis_index("snode"), lax.axis_index("grp")
    x, c = here // (NZ * NC), here % NC
    own = panel[0]
    block = (rows, width)

    wanted = need_list.reshape(-1)
    ids = jnp.arange(NX * NZ * NC * held, dtype=jnp.int32)
    present = jnp.any(wanted[:, None] == ids[None, :], axis=0)
    slot = jnp.sum((present[None, :] & (ids[None, :] < wanted[:, None])).astype(jnp.int32), axis=1)
    order = jnp.arange(SLOTS, dtype=jnp.int32)
    distinct = jnp.max(jnp.where(slot[None, :] == order[:, None], wanted[None, :], 0), axis=1)
    neighbour = lax.ppermute(distinct, "snode", X_ONE)
    twin = lambda v: lax.ppermute(v, "snode", TWIN)
    later, _ = lax.optimization_barrier((own, neighbour))
    twins_own = twin(later)
    pair, twins_own = lax.optimization_barrier((jnp.stack([distinct, neighbour]), twins_own))
    lists = jnp.concatenate([pair, lax.ppermute(pair, "snode", X_TWO)])

    span = held * NC * NZ
    lists = lists[jnp.arange(NX) ^ x]
    begins = jnp.sum((lists[:, None, :] < order[None, : NX + 1, None] * span).astype(jnp.int32), axis=2)
    first = jnp.sum((lists < x * span).astype(jnp.int32), axis=1)
    at = first[:, None] + order[None, :]
    asked = jnp.sum(jnp.where(at[:, :, None] == order, lists[:, None, :], 0), axis=2)
    many = jnp.max(begins[:, 1:] - begins[:, :-1]) > FEW
    owner, k = asked // held, asked % held
    place = owner // NC % NZ * held + k + jnp.where(owner % NC == c, 0, NZ * held)
    place = jnp.where((owner // (NC * NZ) == x) & (at < SLOTS), place, 0)

    copies = pl.pallas_call(
        repeat,
        out_shape=pltpu.HBM((NZ,) + ancestor_inverse.shape, jnp.float32),
        in_specs=[HBM],
        out_specs=HBM,
        scratch_shapes=[
            pltpu.VMEM(ancestor_inverse.shape, jnp.float32),
            pltpu.SemaphoreType.DMA,
            pltpu.SemaphoreType.DMA((NZ,)),
        ],
        compiler_params=PARAMS,
    )(in_hbm(ancestor_inverse))
    mine = lax.all_to_all(
        copies,
        "snode", split_axis=0, concat_axis=0, tiled=True, axis_index_groups=Z_LINES,
    ).reshape((NZ * held,) + block)
    on = lambda v: lax.ppermute(v, ("snode", "grp"), Y_ROUND)
    lead = on(own)
    passed = on(jnp.concatenate([lead, twins_own]))
    mine, place, many, passed = lax.optimization_barrier((mine, place, many, passed))
    twins = twin(mine)
    counts = jnp.sum((distinct[None, :] // span == order[:NX, None]).astype(jnp.int32), axis=1)
    fullest = jnp.argmax(counts).astype(jnp.int32)
    home = wanted // span
    place_there = slot - jnp.sum((distinct[None, :] < home[:, None] * span).astype(jnp.int32), axis=1)
    pick = jnp.where(place_there < FEW, home * FEW, NX * FEW - FEW) + place_there
    staged = pl.pallas_call(
        stage,
        out_shape=pltpu.VMEM((kcount + 1,) + block, jnp.float32),
        in_specs=[VMEM, VMEM],
        out_specs=VMEM,
        compiler_params=PARAMS,
    )(own, diag_factor[0])
    messages = [passed, on(passed)]
    staged, pick, fullest, following = lax.optimization_barrier((staged, pick, fullest, messages[1]))
    messages.append(on(following))
    before, last, _ = lax.optimization_barrier((messages[0], messages[1], following))
    swapped = [twin(before), twin(last), twin(messages[2])]
    pieces = [lead] + messages + swapped
    pieces = [in_vmem(piece) if number in (3, 4) else in_hbm(piece) for number, piece in enumerate(pieces)]

    few, rest = pl.pallas_call(
        collect,
        out_shape=(pltpu.HBM((NX, FEW) + block, jnp.float32), pltpu.HBM((NX, SLOTS - FEW) + block, jnp.float32)),
        in_specs=[SMEM, VMEM, VMEM],
        out_specs=(HBM, HBM),
        scratch_shapes=[pltpu.VMEM((NX, SLOTS) + block, jnp.float32), pltpu.SemaphoreType.DMA((2 * NX,))],
        compiler_params=PARAMS,
        cost_estimate=pl.CostEstimate(flops=0, bytes_accessed=4_000_000, transcendentals=0),
    )(place.reshape(-1), in_vmem(mine), in_vmem(twins))
    over_x = lambda v: lax.all_to_all(
        v, "snode", split_axis=0, concat_axis=0, tiled=True, axis_index_groups=X_LINES
    )
    fetched = over_x(few).reshape((NX * FEW,) + block)
    starts = (y + (2 * c - 1) * jnp.array([0, 1, 2, 3, 4, -1, -2, -3], jnp.int32)) % NY * rows
    whole = pl.pallas_call(
        assemble,
        out_shape=pltpu.VMEM((2, kcount, NY * rows, width), jnp.bfloat16),
        in_specs=[SMEM, VMEM] + [VMEM if number in (3, 4) else HBM for number in range(len(pieces))],
        out_specs=VMEM,
        scratch_shapes=[pltpu.VMEM((NY - 1, kcount) + block, jnp.float32), pltpu.SemaphoreType.DMA((NY - 1,))],
        compiler_params=PARAMS,
        cost_estimate=pl.CostEstimate(flops=0, bytes_accessed=4_000_000, transcendentals=0),
    )(starts, in_vmem(staged), *pieces)
    fetched, rest = lax.optimization_barrier((fetched, rest))
    extra = lax.cond(
        many,
        lambda v: lax.dynamic_index_in_dim(over_x(v), fullest, 0, keepdims=False),
        lambda v: jnp.zeros(v.shape[1:], v.dtype),
        rest,
    )

    off, update = pl.pallas_call(
        products,
        out_shape=(
            pltpu.HBM((kcount,) + block, jnp.float32),
            jax.ShapeDtypeStruct((NY,) + block, jnp.float32),
        ),
        in_specs=[SMEM] * 2 + [VMEM] * 4,
        out_specs=(HBM, VMEM),
        scratch_shapes=[pltpu.VMEM((kcount,) + block, jnp.float32), pltpu.SemaphoreType.DMA],
        compiler_params=PARAMS,
        cost_estimate=pl.CostEstimate(flops=1_000_000_000, bytes_accessed=5_000_000, transcendentals=0),
    )(pick, y.reshape(1), *map(in_vmem, (fetched, extra, staged, whole)))
    parts = lax.all_to_all(update, "grp", split_axis=0, concat_axis=0, tiled=True)
    return off[None], jnp.sum(parts, axis=0)[None]


def solution(mesh):
    return jax.shard_map(
        per_device,
        mesh=mesh,
        in_specs=(
            P("snode", "grp", None),
            P("snode", None, "grp", None),
            P("snode", None, None),
            P("snode", "grp", None),
        ),
        out_specs=(P("snode", None, "grp", None), P("snode", "grp", None)),
        check_vma=False,
    )
```

```python
import jax
import jax.numpy as jnp
from jax import lax
from jax.experimental import pallas as pl
from jax.experimental.pallas import tpu as pltpu
from jax.sharding import PartitionSpec as P

NX, NZ, NC, NY = 4, 8, 2, 8
SLOTS = 16
FEW = 12
HALF = NY // 2


def node(x, z, c):
    return ((x % NX) * NZ + z % NZ) * NC + c


EVERY = [(x, z, c) for x in range(NX) for z in range(NZ) for c in range(NC)]
TWIN = [(node(x, z, c), node(x, z, 1 - c)) for x, z, c in EVERY]
Y_ROUND = [
    (node(x, z, c) * NY + y, node(x, z, c) * NY + (y + 1 - 2 * c) % NY) for x, z, c in EVERY for y in range(NY)
]
X_ONE = [(node(x, z, c), node(x ^ 1, z, c)) for x, z, c in EVERY]
X_TWO = [(node(x, z, c), node(x ^ 2, z, c)) for x, z, c in EVERY]
Z_LINES = [[node(x, z, c) for z in reversed(range(NZ))] for x in range(NX) for c in range(NC)]
X_LINES = [[node(x, z, c) for x in range(NX)] for z in range(NZ) for c in range(NC)]
VMEM = pl.BlockSpec(memory_space=pltpu.VMEM)
HBM = pl.BlockSpec(memory_space=pltpu.HBM)
SMEM = pl.BlockSpec(memory_space=pltpu.SMEM)
in_hbm = lambda v: pltpu.with_memory_space_constraint(v, pltpu.HBM)
in_vmem = lambda v: pltpu.with_memory_space_constraint(v, pltpu.VMEM)
PARAMS = pltpu.CompilerParams(vmem_limit_bytes=12 * 1024 * 1024)


def split(v):
    high = v.astype(jnp.bfloat16)
    return high, (v - high.astype(jnp.float32)).astype(jnp.bfloat16)


def dot3(a, b, dims):
    (ah, al), (bh, bl) = a, b
    dot = lambda u, v: lax.dot_general(u, v, (dims, ((), ())), preferred_element_type=jnp.float32)
    return dot(ah, bh) + (dot(ah, bl) + dot(al, bh))


def repeat(block_ref, all_ref, held_ref, sem, sems):
    copy = pltpu.make_async_copy(block_ref, held_ref, sem)
    copy.start()
    copy.wait()
    copies = [pltpu.make_async_copy(held_ref, all_ref.at[n], sems.at[n]) for n in range(all_ref.shape[0])]
    for copy in copies:
        copy.start()
    for copy in copies:
        copy.wait()


def collect(place_ref, mine_ref, twins_ref, few_ref, rest_ref, picked_ref, sem):
    count = mine_ref.shape[0]
    readers, few = few_ref.shape[:2]
    slots = few + rest_ref.shape[1]
    copies = []
    for target_ref, begin, end in ((few_ref, 0, few), (rest_ref, few, slots)):
        for reader in range(readers):

            def one(s, carry):
                place = place_ref[reader * slots + s]
                inside = lax.rem(place, count)
                picked_ref[reader, s] = jnp.where(place < count, mine_ref[inside], twins_ref[inside])
                return carry

            lax.fori_loop(begin, end, one, 0, unroll=4)
            source = picked_ref.at[reader, pl.ds(begin, end - begin)]
            copies.append(pltpu.make_async_copy(source, target_ref.at[reader], sem.at[len(copies)]))
            copies[-1].start()
    for copy in copies:
        copy.wait()


def stage(own_ref, diag_ref, staged_ref):
    staged_ref[: own_ref.shape[0]] = own_ref[...]
    staged_ref[own_ref.shape[0]] = diag_ref[...]


def assemble(start_ref, staged_ref, *refs):
    *pieces, whole_ref, raw_ref, sems = refs
    _, kcount, width, _ = whole_ref.shape
    rows = width // NY
    messages = (len(pieces) - 1) // 2
    parts = [piece.at[pl.ds(0, kcount)] for piece in pieces[: 1 + messages]]
    parts += [piece.at[pl.ds(kcount, kcount)] for piece in pieces[1 + messages :]]
    copies = [pltpu.make_async_copy(part, raw_ref.at[n], sems.at[n]) for n, part in enumerate(parts)]
    for copy in copies:
        copy.start()
    for number in range(NY):
        if number:
            copies[number - 1].wait()
        start = pl.multiple_of(start_ref[number], rows)
        high, low = split(raw_ref[number - 1] if number else staged_ref[:kcount])
        whole_ref[0, :, pl.ds(start, rows), :] = high
        whole_ref[1, :, pl.ds(start, rows), :] = low


def products(pick_ref, mine_ref, fetched_ref, extra_ref, staged_ref, whole_ref, off_ref, update_ref, held_ref, sem):
    kcount, rows, width = off_ref.shape
    count = fetched_ref.shape[0]

    def named(at):
        usual = fetched_ref[lax.min(at, count - 1)]
        return jnp.where(at < count, usual, extra_ref[lax.max(at - count, 0)])

    total = jnp.zeros((kcount * rows, width), jnp.float32)
    for b in range(kcount):
        left = jnp.concatenate([named(pick_ref[a * kcount + b]) for a in range(kcount)], axis=0)
        total += dot3(split(left), (whole_ref[0, b], whole_ref[1, b]), ((1,), (0,)))
    held_ref[...] = -total.reshape(off_ref.shape)
    copy = pltpu.make_async_copy(held_ref, off_ref, sem)
    copy.start()
    own = staged_ref[:kcount].reshape(total.shape)
    update_ref[...] = dot3(split(own), split(total), ((0,), (0,))).reshape(update_ref.shape)
    update_ref[mine_ref[0]] += staged_ref[kcount]
    copy.wait()


def per_device(ancestor_inverse, panel, need_list, diag_factor):
    _, kcount, rows, width = panel.shape
    held = ancestor_inverse.shape[0]
    here, y = lax.axis_index("snode"), lax.axis_index("grp")
    x, c = here // (NZ * NC), here % NC
    own = panel[0]
    block = (rows, width)

    wanted = need_list.reshape(-1)
    ids = jnp.arange(NX * NZ * NC * held, dtype=jnp.int32)
    present = jnp.any(wanted[:, None] == ids[None, :], axis=0)
    slot = jnp.sum((present[None, :] & (ids[None, :] < wanted[:, None])).astype(jnp.int32), axis=1)
    order = jnp.arange(SLOTS, dtype=jnp.int32)
    distinct = jnp.max(jnp.where(slot[None, :] == order[:, None], wanted[None, :], 0), axis=1)
    neighbour = lax.ppermute(distinct, "snode", X_ONE)
    twin = lambda v: lax.ppermute(v, "snode", TWIN)
    later, _ = lax.optimization_barrier((own, neighbour))
    twins_own = twin(later)
    pair, twins_own = lax.optimization_barrier((jnp.stack([distinct, neighbour]), twins_own))
    lists = jnp.concatenate([pair, lax.ppermute(pair, "snode", X_TWO)])

    span = held * NC * NZ
    lists = lists[jnp.arange(NX) ^ x]
    begins = jnp.sum((lists[:, None, :] < order[None, : NX + 1, None] * span).astype(jnp.int32), axis=2)
    first = jnp.sum((lists < x * span).astype(jnp.int32), axis=1)
    at = first[:, None] + order[None, :]
    asked = jnp.sum(jnp.where(at[:, :, None] == order, lists[:, None, :], 0), axis=2)
    many = jnp.max(begins[:, 1:] - begins[:, :-1]) > FEW
    owner, k = asked // held, asked % held
    place = (NZ - 1 - owner // NC % NZ) * held + k + jnp.where(owner % NC == c, 0, NZ * held)
    place = jnp.where((owner // (NC * NZ) == x) & (at < SLOTS), place, 0)

    copies = pl.pallas_call(
        repeat,
        out_shape=pltpu.HBM((NZ,) + ancestor_inverse.shape, jnp.float32),
        in_specs=[HBM],
        out_specs=HBM,
        scratch_shapes=[
            pltpu.VMEM(ancestor_inverse.shape, jnp.float32),
            pltpu.SemaphoreType.DMA,
            pltpu.SemaphoreType.DMA((NZ,)),
        ],
        compiler_params=PARAMS,
    )(in_hbm(ancestor_inverse))
    mine = lax.all_to_all(
        copies,
        "snode", split_axis=0, concat_axis=0, tiled=True, axis_index_groups=Z_LINES,
    ).reshape((NZ * held,) + block)
    on = lambda v: lax.ppermute(v, ("snode", "grp"), Y_ROUND)
    lead = on(own)
    passed = on(jnp.concatenate([lead, twins_own]))
    mine, place, many, passed = lax.optimization_barrier((mine, place, many, passed))
    twins = twin(mine)
    counts = jnp.sum((distinct[None, :] // span == order[:NX, None]).astype(jnp.int32), axis=1)
    fullest = jnp.argmax(counts).astype(jnp.int32)
    home = wanted // span
    place_there = slot - jnp.sum((distinct[None, :] < home[:, None] * span).astype(jnp.int32), axis=1)
    pick = jnp.where(place_there < FEW, home * FEW, NX * FEW - FEW) + place_there
    staged = pl.pallas_call(
        stage,
        out_shape=pltpu.VMEM((kcount + 1,) + block, jnp.float32),
        in_specs=[VMEM, VMEM],
        out_specs=VMEM,
        compiler_params=PARAMS,
    )(own, diag_factor[0])
    messages = [passed, on(passed)]
    staged, pick, fullest, following = lax.optimization_barrier((staged, pick, fullest, messages[1]))
    messages.append(on(following))
    before, last, _ = lax.optimization_barrier((messages[0], messages[1], following))
    swapped = [twin(before), twin(last), twin(messages[2])]
    pieces = [lead] + messages + swapped
    pieces = [in_vmem(piece) if number in (3, 4) else in_hbm(piece) for number, piece in enumerate(pieces)]

    few, rest = pl.pallas_call(
        collect,
        out_shape=(pltpu.HBM((NX, FEW) + block, jnp.float32), pltpu.HBM((NX, SLOTS - FEW) + block, jnp.float32)),
        in_specs=[SMEM, VMEM, VMEM],
        out_specs=(HBM, HBM),
        scratch_shapes=[pltpu.VMEM((NX, SLOTS) + block, jnp.float32), pltpu.SemaphoreType.DMA((2 * NX,))],
        compiler_params=PARAMS,
        cost_estimate=pl.CostEstimate(flops=0, bytes_accessed=4_000_000, transcendentals=0),
    )(place.reshape(-1), in_vmem(mine), in_vmem(twins))
    over_x = lambda v: lax.all_to_all(
        v, "snode", split_axis=0, concat_axis=0, tiled=True, axis_index_groups=X_LINES
    )
    fetched = over_x(few).reshape((NX * FEW,) + block)
    starts = (y + (2 * c - 1) * jnp.array([0, 1, 2, 3, 4, -1, -2, -3], jnp.int32)) % NY * rows
    whole = pl.pallas_call(
        assemble,
        out_shape=pltpu.VMEM((2, kcount, NY * rows, width), jnp.bfloat16),
        in_specs=[SMEM, VMEM] + [VMEM if number in (3, 4) else HBM for number in range(len(pieces))],
        out_specs=VMEM,
        scratch_shapes=[pltpu.VMEM((NY - 1, kcount) + block, jnp.float32), pltpu.SemaphoreType.DMA((NY - 1,))],
        compiler_params=PARAMS,
        cost_estimate=pl.CostEstimate(flops=0, bytes_accessed=4_000_000, transcendentals=0),
    )(starts, in_vmem(staged), *pieces)
    fetched, rest = lax.optimization_barrier((fetched, rest))
    extra = lax.cond(
        many,
        lambda v: lax.dynamic_index_in_dim(over_x(v), fullest, 0, keepdims=False),
        lambda v: jnp.zeros(v.shape[1:], v.dtype),
        rest,
    )

    off, update = pl.pallas_call(
        products,
        out_shape=(
            pltpu.HBM((kcount,) + block, jnp.float32),
            jax.ShapeDtypeStruct((NY,) + block, jnp.float32),
        ),
        in_specs=[SMEM] * 2 + [VMEM] * 4,
        out_specs=(HBM, VMEM),
        scratch_shapes=[pltpu.VMEM((kcount,) + block, jnp.float32), pltpu.SemaphoreType.DMA],
        compiler_params=PARAMS,
        cost_estimate=pl.CostEstimate(flops=1_000_000_000, bytes_accessed=5_000_000, transcendentals=0),
    )(pick, y.reshape(1), *map(in_vmem, (fetched, extra, staged, whole)))
    parts = lax.all_to_all(update, "grp", split_axis=0, concat_axis=0, tiled=True)
    return off[None], jnp.sum(parts, axis=0)[None]


def solution(mesh):
    return jax.shard_map(
        per_device,
        mesh=mesh,
        in_specs=(
            P("snode", "grp", None),
            P("snode", None, "grp", None),
            P("snode", None, None),
            P("snode", "grp", None),
        ),
        out_specs=(P("snode", None, "grp", None), P("snode", "grp", None)),
        check_vma=False,
    )
```

```python
import jax
import jax.numpy as jnp
from jax import lax
from jax.experimental import pallas as pl
from jax.experimental.pallas import tpu as pltpu
from jax.sharding import PartitionSpec as P

NX, NZ, NC, NY = 4, 8, 2, 8
SLOTS = 16
FEW = 12
HALF = NY // 2


def node(x, z, c):
    return ((x % NX) * NZ + z % NZ) * NC + c


EVERY = [(x, z, c) for x in range(NX) for z in range(NZ) for c in range(NC)]
TWIN = [(node(x, z, c), node(x, z, 1 - c)) for x, z, c in EVERY]
Y_ROUND = [
    (node(x, z, c) * NY + y, node(x, z, c) * NY + (y + 1 - 2 * c) % NY) for x, z, c in EVERY for y in range(NY)
]
X_ONE = [(node(x, z, c), node(x ^ 1, z, c)) for x, z, c in EVERY]
X_TWO = [(node(x, z, c), node(x ^ 2, z, c)) for x, z, c in EVERY]
Z_LINES = [[node(x, z, c) for z in range(NZ)] for x in range(NX) for c in range(NC)]
X_LINES = [[node(x, z, c) for x in range(NX)] for z in range(NZ) for c in range(NC)]
VMEM = pl.BlockSpec(memory_space=pltpu.VMEM)
HBM = pl.BlockSpec(memory_space=pltpu.HBM)
SMEM = pl.BlockSpec(memory_space=pltpu.SMEM)
in_hbm = lambda v: pltpu.with_memory_space_constraint(v, pltpu.HBM)
in_vmem = lambda v: pltpu.with_memory_space_constraint(v, pltpu.VMEM)
PARAMS = pltpu.CompilerParams(vmem_limit_bytes=12 * 1024 * 1024)


def split(v):
    high = v.astype(jnp.bfloat16)
    return high, (v - high.astype(jnp.float32)).astype(jnp.bfloat16)


def dot3(a, b, dims):
    (ah, al), (bh, bl) = a, b
    dot = lambda u, v: lax.dot_general(u, v, (dims, ((), ())), preferred_element_type=jnp.float32)
    return dot(ah, bh) + (dot(ah, bl) + dot(al, bh))


def repeat(block_ref, all_ref, held_ref, sem, sems):
    copy = pltpu.make_async_copy(block_ref, held_ref, sem)
    copy.start()
    copy.wait()
    copies = [pltpu.make_async_copy(held_ref, all_ref.at[n], sems.at[n]) for n in range(all_ref.shape[0])]
    for copy in copies:
        copy.start()
    for copy in copies:
        copy.wait()


def collect(place_ref, mine_ref, twins_ref, few_ref, rest_ref, picked_ref, sem):
    count = mine_ref.shape[0]
    readers, few = few_ref.shape[:2]
    slots = few + rest_ref.shape[1]
    copies = []
    for target_ref, begin, end in ((few_ref, 0, few), (rest_ref, few, slots)):
        for reader in range(readers):

            def one(s, carry):
                place = place_ref[reader * slots + s]
                inside = lax.rem(place, count)
                picked_ref[reader, s] = jnp.where(place < count, mine_ref[inside], twins_ref[inside])
                return carry

            lax.fori_loop(begin, end, one, 0, unroll=4)
            source = picked_ref.at[reader, pl.ds(begin, end - begin)]
            copies.append(pltpu.make_async_copy(source, target_ref.at[reader], sem.at[len(copies)]))
            copies[-1].start()
    for copy in copies:
        copy.wait()


def stage(own_ref, diag_ref, staged_ref):
    staged_ref[: own_ref.shape[0]] = own_ref[...]
    staged_ref[own_ref.shape[0]] = diag_ref[...]


def assemble(start_ref, staged_ref, *refs):
    *pieces, whole_ref, raw_ref, sems = refs
    _, kcount, width, _ = whole_ref.shape
    rows = width // NY
    messages = (len(pieces) - 1) // 2
    parts = [piece.at[pl.ds(0, kcount)] for piece in pieces[: 1 + messages]]
    parts += [piece.at[pl.ds(kcount, kcount)] for piece in pieces[1 + messages :]]
    copies = [pltpu.make_async_copy(part, raw_ref.at[n], sems.at[n]) for n, part in enumerate(parts)]
    for copy in copies:
        copy.start()
    for number in range(NY):
        if number:
            copies[number - 1].wait()
        start = pl.multiple_of(start_ref[number], rows)
        high, low = split(raw_ref[number - 1] if number else staged_ref[:kcount])
        whole_ref[0, :, pl.ds(start, rows), :] = high
        whole_ref[1, :, pl.ds(start, rows), :] = low


def products(pick_ref, mine_ref, fetched_ref, extra_ref, staged_ref, whole_ref, off_ref, update_ref, held_ref, sem):
    kcount, rows, width = off_ref.shape
    count = fetched_ref.shape[0]

    def named(at):
        usual = fetched_ref[lax.min(at, count - 1)]
        return jnp.where(at < count, usual, extra_ref[lax.max(at - count, 0)])

    total = jnp.zeros((kcount * rows, width), jnp.float32)
    for b in range(kcount):
        left = jnp.concatenate([named(pick_ref[a * kcount + b]) for a in range(kcount)], axis=0)
        total += dot3(split(left), (whole_ref[0, b], whole_ref[1, b]), ((1,), (0,)))
    held_ref[...] = -total.reshape(off_ref.shape)
    copy = pltpu.make_async_copy(held_ref, off_ref, sem)
    copy.start()
    own = staged_ref[:kcount].reshape(total.shape)
    update_ref[...] = dot3(split(own), split(total), ((0,), (0,))).reshape(update_ref.shape)
    update_ref[mine_ref[0]] += staged_ref[kcount]
    copy.wait()


def per_device(ancestor_inverse, panel, need_list, diag_factor):
    _, kcount, rows, width = panel.shape
    held = ancestor_inverse.shape[0]
    here, y = lax.axis_index("snode"), lax.axis_index("grp")
    x, c = here // (NZ * NC), here % NC
    own = panel[0]
    block = (rows, width)

    wanted = need_list.reshape(-1)
    ids = jnp.arange(NX * NZ * NC * held, dtype=jnp.int32)
    present = jnp.any(wanted[:, None] == ids[None, :], axis=0)
    slot = jnp.sum((present[None, :] & (ids[None, :] < wanted[:, None])).astype(jnp.int32), axis=1)
    order = jnp.arange(SLOTS, dtype=jnp.int32)
    distinct = jnp.max(jnp.where(slot[None, :] == order[:, None], wanted[None, :], 0), axis=1)
    neighbour = lax.ppermute(distinct, "snode", X_ONE)
    twin = lambda v: lax.ppermute(v, "snode", TWIN)
    later, _ = lax.optimization_barrier((own, neighbour))
    twins_own = twin(later)
    pair, twins_own = lax.optimization_barrier((jnp.stack([distinct, neighbour]), twins_own))
    lists = jnp.concatenate([pair, lax.ppermute(pair, "snode", X_TWO)])

    span = held * NC * NZ
    lists = lists[jnp.arange(NX) ^ x]
    begins = jnp.sum((lists[:, None, :] < order[None, : NX + 1, None] * span).astype(jnp.int32), axis=2)
    first = jnp.sum((lists < x * span).astype(jnp.int32), axis=1)
    at = first[:, None] + order[None, :]
    asked = jnp.sum(jnp.where(at[:, :, None] == order, lists[:, None, :], 0), axis=2)
    many = jnp.max(begins[:, 1:] - begins[:, :-1]) > FEW
    owner, k = asked // held, asked % held
    place = owner // NC % NZ * held + k + jnp.where(owner % NC == c, 0, NZ * held)
    place = jnp.where((owner // (NC * NZ) == x) & (at < SLOTS), place, 0)

    copies = pl.pallas_call(
        repeat,
        out_shape=pltpu.HBM((NZ,) + ancestor_inverse.shape, jnp.float32),
        in_specs=[HBM],
        out_specs=HBM,
        scratch_shapes=[
            pltpu.VMEM(ancestor_inverse.shape, jnp.float32),
            pltpu.SemaphoreType.DMA,
            pltpu.SemaphoreType.DMA((NZ,)),
        ],
        compiler_params=PARAMS,
    )(in_hbm(ancestor_inverse))
    mine = lax.all_to_all(
        copies,
        "snode", split_axis=0, concat_axis=0, tiled=True, axis_index_groups=Z_LINES,
    ).reshape((NZ * held,) + block)
    on = lambda v: lax.ppermute(v, ("snode", "grp"), Y_ROUND)
    lead = on(own)
    passed = on(jnp.concatenate([lead, twins_own]))
    mine, place, many, passed = lax.optimization_barrier((mine, place, many, passed))
    twins = twin(mine)
    home = wanted // span
    place_there = slot - jnp.sum((distinct[None, :] < home[:, None] * span).astype(jnp.int32), axis=1)
    pick = jnp.where(place_there < FEW, home * FEW, NX * FEW - FEW) + place_there
    staged = pl.pallas_call(
        stage,
        out_shape=pltpu.VMEM((kcount + 1,) + block, jnp.float32),
        in_specs=[VMEM, VMEM],
        out_specs=VMEM,
        compiler_params=PARAMS,
    )(own, diag_factor[0])
    messages = [passed, on(passed)]
    staged, pick, following = lax.optimization_barrier((staged, pick, messages[1]))
    messages.append(on(following))
    before, last, _ = lax.optimization_barrier((messages[0], messages[1], following))
    swapped = [twin(before), twin(last), twin(messages[2])]
    pieces = [lead] + messages + swapped
    pieces = [in_vmem(piece) if number in (3, 4) else in_hbm(piece) for number, piece in enumerate(pieces)]

    few, rest = pl.pallas_call(
        collect,
        out_shape=(pltpu.HBM((NX, FEW) + block, jnp.float32), pltpu.HBM((NX, SLOTS - FEW) + block, jnp.float32)),
        in_specs=[SMEM, VMEM, VMEM],
        out_specs=(HBM, HBM),
        scratch_shapes=[pltpu.VMEM((NX, SLOTS) + block, jnp.float32), pltpu.SemaphoreType.DMA((2 * NX,))],
        compiler_params=PARAMS,
        cost_estimate=pl.CostEstimate(flops=0, bytes_accessed=4_000_000, transcendentals=0),
    )(place.reshape(-1), in_vmem(mine), in_vmem(twins))
    over_x = lambda v: lax.all_to_all(
        v, "snode", split_axis=0, concat_axis=0, tiled=True, axis_index_groups=X_LINES
    )
    fetched = over_x(few).reshape((NX * FEW,) + block)
    starts = (y + (2 * c - 1) * jnp.array([0, 1, 2, 3, 4, -1, -2, -3], jnp.int32)) % NY * rows
    whole = pl.pallas_call(
        assemble,
        out_shape=pltpu.VMEM((2, kcount, NY * rows, width), jnp.bfloat16),
        in_specs=[SMEM, VMEM] + [VMEM if number in (3, 4) else HBM for number in range(len(pieces))],
        out_specs=VMEM,
        scratch_shapes=[pltpu.VMEM((NY - 1, kcount) + block, jnp.float32), pltpu.SemaphoreType.DMA((NY - 1,))],
        compiler_params=PARAMS,
        cost_estimate=pl.CostEstimate(flops=0, bytes_accessed=4_000_000, transcendentals=0),
    )(starts, in_vmem(staged), *pieces)
    _, rest = lax.optimization_barrier((fetched, rest))

    def more(rest, distinct):
        counts = jnp.sum((distinct[None, :] // span == order[:NX, None]).astype(jnp.int32), axis=1)
        return lax.dynamic_index_in_dim(over_x(rest), jnp.argmax(counts), 0, keepdims=False)

    extra = lax.cond(many, more, lambda rest, _: jnp.zeros(rest.shape[1:], rest.dtype), rest, distinct)

    off, update = pl.pallas_call(
        products,
        out_shape=(
            pltpu.HBM((kcount,) + block, jnp.float32),
            jax.ShapeDtypeStruct((NY,) + block, jnp.float32),
        ),
        in_specs=[SMEM] * 2 + [VMEM] * 4,
        out_specs=(HBM, VMEM),
        scratch_shapes=[pltpu.VMEM((kcount,) + block, jnp.float32), pltpu.SemaphoreType.DMA],
        compiler_params=PARAMS,
        cost_estimate=pl.CostEstimate(flops=1_000_000_000, bytes_accessed=5_000_000, transcendentals=0),
    )(pick, y.reshape(1), *map(in_vmem, (fetched, extra, staged, whole)))
    parts = lax.all_to_all(update, "grp", split_axis=0, concat_axis=0, tiled=True)
    return off[None], jnp.sum(parts, axis=0)[None]


def solution(mesh):
    return jax.shard_map(
        per_device,
        mesh=mesh,
        in_specs=(
            P("snode", "grp", None),
            P("snode", None, "grp", None),
            P("snode", None, None),
            P("snode", "grp", None),
        ),
        out_specs=(P("snode", None, "grp", None), P("snode", "grp", None)),
        check_vma=False,
    )
```

```python
import jax
import jax.numpy as jnp
from jax import lax
from jax.experimental import pallas as pl
from jax.experimental.pallas import tpu as pltpu
from jax.sharding import PartitionSpec as P

NX, NZ, NC, NY = 4, 8, 2, 8
SLOTS = 16
FEW = 12
HALF = NY // 2


def node(x, z, c):
    return ((x % NX) * NZ + z % NZ) * NC + c


EVERY = [(x, z, c) for x in range(NX) for z in range(NZ) for c in range(NC)]
TWIN = [(node(x, z, c), node(x, z, 1 - c)) for x, z, c in EVERY]
Y_ROUND = [
    (node(x, z, c) * NY + y, node(x, z, c) * NY + (y + 1 - 2 * c) % NY) for x, z, c in EVERY for y in range(NY)
]
X_ONE = [(node(x, z, c), node(x ^ 1, z, c)) for x, z, c in EVERY]
X_TWO = [(node(x, z, c), node(x ^ 2, z, c)) for x, z, c in EVERY]
Z_LINES = [[node(x, z, c) for z in range(NZ)] for x in range(NX) for c in range(NC)]
X_LINES = [[node(x, z, c) for x in range(NX)] for z in range(NZ) for c in range(NC)]
VMEM = pl.BlockSpec(memory_space=pltpu.VMEM)
HBM = pl.BlockSpec(memory_space=pltpu.HBM)
SMEM = pl.BlockSpec(memory_space=pltpu.SMEM)
in_hbm = lambda v: pltpu.with_memory_space_constraint(v, pltpu.HBM)
in_vmem = lambda v: pltpu.with_memory_space_constraint(v, pltpu.VMEM)
PARAMS = pltpu.CompilerParams(vmem_limit_bytes=12 * 1024 * 1024)


def split(v):
    high = v.astype(jnp.bfloat16)
    return high, (v - high.astype(jnp.float32)).astype(jnp.bfloat16)


def dot3(a, b, dims):
    (ah, al), (bh, bl) = a, b
    dot = lambda u, v: lax.dot_general(u, v, (dims, ((), ())), preferred_element_type=jnp.float32)
    return dot(ah, bh) + (dot(ah, bl) + dot(al, bh))


def repeat(block_ref, all_ref, held_ref, sem, sems):
    copy = pltpu.make_async_copy(block_ref, held_ref, sem)
    copy.start()
    copy.wait()
    copies = [pltpu.make_async_copy(held_ref, all_ref.at[n], sems.at[n]) for n in range(all_ref.shape[0])]
    for copy in copies:
        copy.start()
    for copy in copies:
        copy.wait()


def collect(place_ref, mine_ref, twins_ref, few_ref, rest_ref, picked_ref, sem):
    count = mine_ref.shape[0]
    readers, few = few_ref.shape[:2]
    slots = few + rest_ref.shape[1]
    copies = []
    for target_ref, begin, end in ((few_ref, 0, few), (rest_ref, few, slots)):
        for reader in range(readers):

            def one(s, carry):
                place = place_ref[reader * slots + s]
                inside = lax.rem(place, count)
                picked_ref[reader, s] = jnp.where(place < count, mine_ref[inside], twins_ref[inside])
                return carry

            lax.fori_loop(begin, end, one, 0, unroll=4)
            source = picked_ref.at[reader, pl.ds(begin, end - begin)]
            copies.append(pltpu.make_async_copy(source, target_ref.at[reader], sem.at[len(copies)]))
            copies[-1].start()
    for copy in copies:
        copy.wait()


def stage(own_ref, diag_ref, staged_ref):
    staged_ref[: own_ref.shape[0]] = own_ref[...]
    staged_ref[own_ref.shape[0]] = diag_ref[...]


def place_rows(whole_ref, start, rows, piece):
    start = pl.multiple_of(start, rows)
    high, low = split(piece)
    whole_ref[0, :, pl.ds(start, rows), :] = high
    whole_ref[1, :, pl.ds(start, rows), :] = low


def assemble(start_ref, staged_ref, *refs):
    *pieces, whole_ref, raw_ref, sems = refs
    _, kcount, width, _ = whole_ref.shape
    rows = width // NY
    leads = (len(pieces) + 1) // 2
    parts = [piece.at[pl.ds(0 if n < leads else kcount, kcount)] for n, piece in enumerate(pieces)]
    copies = [pltpu.make_async_copy(part, raw_ref.at[n], sems.at[n]) for n, part in enumerate(parts)]
    for copy in copies:
        copy.start()
    place_rows(whole_ref, start_ref[0], rows, staged_ref[:kcount])
    for number, copy in enumerate(copies):
        copy.wait()
        place_rows(whole_ref, start_ref[number + 1], rows, raw_ref[number])


def complete(start_ref, lead_ref, lag_ref, _, whole_ref):
    _, kcount, width, _ = whole_ref.shape
    rows = width // NY
    place_rows(whole_ref, start_ref[NY - 2], rows, lead_ref[:kcount])
    place_rows(whole_ref, start_ref[NY - 1], rows, lag_ref[kcount:])


def products(pick_ref, mine_ref, fetched_ref, extra_ref, staged_ref, whole_ref, off_ref, update_ref, held_ref, sem):
    kcount, rows, width = off_ref.shape
    count = fetched_ref.shape[0]

    def named(at):
        usual = fetched_ref[lax.min(at, count - 1)]
        return jnp.where(at < count, usual, extra_ref[lax.max(at - count, 0)])

    total = jnp.zeros((kcount * rows, width), jnp.float32)
    for b in range(kcount):
        left = jnp.concatenate([named(pick_ref[a * kcount + b]) for a in range(kcount)], axis=0)
        total += dot3(split(left), (whole_ref[0, b], whole_ref[1, b]), ((1,), (0,)))
    held_ref[...] = -total.reshape(off_ref.shape)
    copy = pltpu.make_async_copy(held_ref, off_ref, sem)
    copy.start()
    own = staged_ref[:kcount].reshape(total.shape)
    update_ref[...] = dot3(split(own), split(total), ((0,), (0,))).reshape(update_ref.shape)
    update_ref[mine_ref[0]] += staged_ref[kcount]
    copy.wait()


def per_device(ancestor_inverse, panel, need_list, diag_factor):
    _, kcount, rows, width = panel.shape
    held = ancestor_inverse.shape[0]
    here, y = lax.axis_index("snode"), lax.axis_index("grp")
    x, c = here // (NZ * NC), here % NC
    own = panel[0]
    block = (rows, width)

    wanted = need_list.reshape(-1)
    ids = jnp.arange(NX * NZ * NC * held, dtype=jnp.int32)
    present = jnp.any(wanted[:, None] == ids[None, :], axis=0)
    slot = jnp.sum((present[None, :] & (ids[None, :] < wanted[:, None])).astype(jnp.int32), axis=1)
    order = jnp.arange(SLOTS, dtype=jnp.int32)
    distinct = jnp.max(jnp.where(slot[None, :] == order[:, None], wanted[None, :], 0), axis=1)
    neighbour = lax.ppermute(distinct, "snode", X_ONE)
    twin = lambda v: lax.ppermute(v, "snode", TWIN)
    later, _ = lax.optimization_barrier((own, neighbour))
    twins_own = twin(later)
    pair, twins_own = lax.optimization_barrier((jnp.stack([distinct, neighbour]), twins_own))
    lists = jnp.concatenate([pair, lax.ppermute(pair, "snode", X_TWO)])

    span = held * NC * NZ
    lists = lists[jnp.arange(NX) ^ x]
    begins = jnp.sum((lists[:, None, :] < order[None, : NX + 1, None] * span).astype(jnp.int32), axis=2)
    first = jnp.sum((lists < x * span).astype(jnp.int32), axis=1)
    at = first[:, None] + order[None, :]
    asked = jnp.sum(jnp.where(at[:, :, None] == order, lists[:, None, :], 0), axis=2)
    many = jnp.max(begins[:, 1:] - begins[:, :-1]) > FEW
    owner, k = asked // held, asked % held
    place = owner // NC % NZ * held + k + jnp.where(owner % NC == c, 0, NZ * held)
    place = jnp.where((owner // (NC * NZ) == x) & (at < SLOTS), place, 0)

    copies = pl.pallas_call(
        repeat,
        out_shape=pltpu.HBM((NZ,) + ancestor_inverse.shape, jnp.float32),
        in_specs=[HBM],
        out_specs=HBM,
        scratch_shapes=[
            pltpu.VMEM(ancestor_inverse.shape, jnp.float32),
            pltpu.SemaphoreType.DMA,
            pltpu.SemaphoreType.DMA((NZ,)),
        ],
        compiler_params=PARAMS,
    )(in_hbm(ancestor_inverse))
    mine = lax.all_to_all(
        copies,
        "snode", split_axis=0, concat_axis=0, tiled=True, axis_index_groups=Z_LINES,
    ).reshape((NZ * held,) + block)
    on = lambda v: lax.ppermute(v, ("snode", "grp"), Y_ROUND)
    lead = on(own)
    passed = on(jnp.concatenate([lead, twins_own]))
    mine, place, many, passed = lax.optimization_barrier((mine, place, many, passed))
    twins = twin(mine)
    home = wanted // span
    place_there = slot - jnp.sum((distinct[None, :] < home[:, None] * span).astype(jnp.int32), axis=1)
    pick = jnp.where(place_there < FEW, home * FEW, NX * FEW - FEW) + place_there
    staged = pl.pallas_call(
        stage,
        out_shape=pltpu.VMEM((kcount + 1,) + block, jnp.float32),
        in_specs=[VMEM, VMEM],
        out_specs=VMEM,
        compiler_params=PARAMS,
    )(own, diag_factor[0])
    messages = [passed, on(passed)]
    staged, pick, following = lax.optimization_barrier((staged, pick, messages[1]))
    messages.append(on(following))
    before, last, _ = lax.optimization_barrier((messages[0], messages[1], following))
    swapped = [twin(before), twin(last), twin(messages[2])]
    pieces = [in_hbm(piece) for piece in [lead, *messages[:2], *swapped[:2]]]

    few, rest = pl.pallas_call(
        collect,
        out_shape=(pltpu.HBM((NX, FEW) + block, jnp.float32), pltpu.HBM((NX, SLOTS - FEW) + block, jnp.float32)),
        in_specs=[SMEM, VMEM, VMEM],
        out_specs=(HBM, HBM),
        scratch_shapes=[pltpu.VMEM((NX, SLOTS) + block, jnp.float32), pltpu.SemaphoreType.DMA((2 * NX,))],
        compiler_params=PARAMS,
        cost_estimate=pl.CostEstimate(flops=0, bytes_accessed=4_000_000, transcendentals=0),
    )(place.reshape(-1), in_vmem(mine), in_vmem(twins))
    over_x = lambda v: lax.all_to_all(
        v, "snode", split_axis=0, concat_axis=0, tiled=True, axis_index_groups=X_LINES
    )
    fetched = over_x(few).reshape((NX * FEW,) + block)
    starts = (y + (2 * c - 1) * jnp.array([0, 1, 2, 3, -1, -2, 4, -3], jnp.int32)) % NY * rows
    whole_shape = pltpu.VMEM((2, kcount, NY * rows, width), jnp.bfloat16)
    whole = pl.pallas_call(
        assemble,
        out_shape=whole_shape,
        in_specs=[SMEM, VMEM] + [HBM] * len(pieces),
        out_specs=VMEM,
        scratch_shapes=[
            pltpu.VMEM((len(pieces), kcount) + block, jnp.float32),
            pltpu.SemaphoreType.DMA((len(pieces),)),
        ],
        compiler_params=PARAMS,
        cost_estimate=pl.CostEstimate(flops=0, bytes_accessed=4_000_000, transcendentals=0),
    )(starts, in_vmem(staged), *pieces)
    whole = pl.pallas_call(
        complete,
        out_shape=whole_shape,
        in_specs=[SMEM] + [VMEM] * 3,
        out_specs=VMEM,
        input_output_aliases={3: 0},
        compiler_params=PARAMS,
        cost_estimate=pl.CostEstimate(flops=0, bytes_accessed=1_000_000, transcendentals=0),
    )(starts, in_vmem(messages[2]), in_vmem(swapped[2]), in_vmem(whole))
    _, rest = lax.optimization_barrier((fetched, rest))

    def more(rest, distinct):
        counts = jnp.sum((distinct[None, :] // span == order[:NX, None]).astype(jnp.int32), axis=1)
        return lax.dynamic_index_in_dim(over_x(rest), jnp.argmax(counts), 0, keepdims=False)

    extra = lax.cond(many, more, lambda rest, _: jnp.zeros(rest.shape[1:], rest.dtype), rest, distinct)

    off, update = pl.pallas_call(
        products,
        out_shape=(
            pltpu.HBM((kcount,) + block, jnp.float32),
            jax.ShapeDtypeStruct((NY,) + block, jnp.float32),
        ),
        in_specs=[SMEM] * 2 + [VMEM] * 4,
        out_specs=(HBM, VMEM),
        scratch_shapes=[pltpu.VMEM((kcount,) + block, jnp.float32), pltpu.SemaphoreType.DMA],
        compiler_params=PARAMS,
        cost_estimate=pl.CostEstimate(flops=1_000_000_000, bytes_accessed=5_000_000, transcendentals=0),
    )(pick, y.reshape(1), *map(in_vmem, (fetched, extra, staged, whole)))
    parts = lax.all_to_all(update, "grp", split_axis=0, concat_axis=0, tiled=True)
    return off[None], jnp.sum(parts, axis=0)[None]


def solution(mesh):
    return jax.shard_map(
        per_device,
        mesh=mesh,
        in_specs=(
            P("snode", "grp", None),
            P("snode", None, "grp", None),
            P("snode", None, None),
            P("snode", "grp", None),
        ),
        out_specs=(P("snode", None, "grp", None), P("snode", "grp", None)),
        check_vma=False,
    )
```
